32 devices in a mesh: grp: 2 (over y), row: 4 (over z), col: 2 (over x), rep: 2 (over core).
Axes of the slice: x: 2, y: 2, z: 4, core: 2. Of those that a mesh axis runs over, the one named last changes fastest.
Arguments:
- features: bfloat16 [64, 65536], P(('grp', 'row'), ('col', 'rep')), parts along dimension 0, may hold values from 0 to 1
- tiles: bfloat16 [2, 4, 128, 4, 3, 128, 128], P(None, None, 'row', ('col', 'rep')), may hold values from -0.29882812 to 0.29882812
- tile_rows: int32 [2, 4, 128, 4, 3], P(None, None, 'row', ('col', 'rep')), may hold values from 0 to 127
- tile_counts: int32 [2, 4, 128, 4], P(None, None, 'row', ('col', 'rep')), may hold values from 0 to 3, as said below
- bias: float32 [2, 65536], P(None, ('col', 'rep')), may hold values from -0.3 to 0.3
Outputs:
- activations: bfloat16 [64, 65536], P(('grp', 'row'), ('col', 'rep')), parts along dimension 0
The draws below stay inside these ranges and needn't reach their ends.
There are 2 independent parts, one for each index of `grp`. The reference program is written for one: setup_inputs(seed, part) draws one part's arguments, and reference() takes and returns one part's arrays. A program takes and returns all parts, laid end to end along the dimension named above; an argument that names none is the same for every part. Nothing has to cross between parts.
Inputs may be any that keep to these rules, and one draw needn't show every extreme that they name: `tile_counts`: in every layer each block column has exactly 3 live slots in one input piece and fewer in the others.
All inputs are finite; a program needn't handle non-finite values.
Results may differ from the reference program's by a relative error of at most 0.005.
Values may be sent and summed in bfloat16 or wider, within the bound.
A program may use at most 128 MiB of HBM per device.

```python
import jax
import jax.numpy as jnp
from jax import lax

NEURONS = 65536
TILE = 128
LAYERS = 2
MAXS = 3
ROWS = 32
PIECES = 4
PB = 128


def draw_tile_counts(key, part):
    key = jax.random.fold_in(key, 7)
    base_key, heavy_key = jax.random.split(key)
    base = jax.random.randint(base_key, (LAYERS, PIECES, PB, PIECES), 0, MAXS)
    heavy = jax.random.randint(heavy_key, (LAYERS, PIECES, PB), 0, PIECES)
    position = jnp.arange(PIECES, dtype=jnp.int32)
    return jnp.where(position[None, None, None, :] == heavy[..., None], MAXS, base).astype(jnp.int32)


def plant(result, own_key, low, largest):
    shape = result.shape
    index_at = [jax.random.randint(jax.random.fold_in(own_key, axis), (), 0, shape[axis]) for axis in range(len(shape))]
    result = result.at[tuple(index_at)].set(low)
    longest = shape.index(max(shape))
    index_at[longest] = (index_at[longest] + 1) % shape[longest]
    return result.at[tuple(index_at)].set(largest)


def block_scale(key, extent, cuts, smallest, largest):
    level, own = 1.0, jax.random.fold_in(key, 6)
    for dim, blocks in cuts:
        heights = jnp.exp(jax.random.uniform(jax.random.fold_in(own, dim), (blocks,), jnp.float32, smallest / len(cuts), largest / len(cuts)))
        level = level * jnp.repeat(heights, extent[dim] // blocks).reshape([-1 if axis == dim else 1 for axis in range(len(extent))])
    return level


def centred(stream_key, extent, deviation, reach, pieces=(), held_as=jnp.bfloat16):
    loudness = block_scale(stream_key, extent, pieces, -0.22, 0.18) if pieces else 1.0
    values = jax.random.normal(stream_key, extent, jnp.float32) * deviation * loudness
    return jnp.minimum(jnp.maximum(values, -reach), reach).astype(held_as)


def setup_inputs(seed: int = 0, part: int = 0) -> dict:
    seeds = jax.random.split(jax.random.key(seed), 6)
    own_keys = jax.random.split(jax.random.fold_in(seeds[5], part), 6)
    features = jnp.clip(1.0 * jax.random.uniform(own_keys[0], (ROWS, NEURONS), jnp.float32) ** block_scale(own_keys[0], (ROWS, NEURONS), ((0, 4), (1, 4)), -0.2, 0.2), 0.0, 1.0).astype(jnp.bfloat16)
    tiles = centred(seeds[1], (LAYERS, PIECES, PB, PIECES, MAXS, TILE, TILE), 0.05, 0.29882812, ((2, 4), (3, 4)))
    tile_rows = plant(jax.random.randint(seeds[2], (LAYERS, PIECES, PB, PIECES, MAXS), 0, PB), jax.random.fold_in(seeds[2], 1), 0, PB - 1).astype(jnp.int32)
    tile_counts = draw_tile_counts(jax.random.fold_in(seeds[5], 71), part)
    bias = jnp.clip(jax.random.uniform(seeds[4], (LAYERS, NEURONS), jnp.float32, -0.3, 0.3) * block_scale(seeds[4], (LAYERS, NEURONS), ((1, 4),), -0.4, 0.0), -0.3, 0.3)
    return {"features": features, "tiles": tiles, "tile_rows": tile_rows, "tile_counts": tile_counts, "bias": bias}


def one_layer(inputs, weights, rows_idx, counts, shifts):
    height = inputs.shape[0]
    blocks = inputs.reshape(height, PIECES, PB, TILE)

    def per_output(packed):
        weight_o, index_o, count_o = packed
        total = jnp.zeros((height, PB, TILE), jnp.float32)
        for piece in range(PIECES):
            source = blocks[:, piece]
            picked = jnp.take(source, index_o[:, piece], axis=1).astype(jnp.float32)
            live = (jnp.arange(MAXS)[None, :] < count_o[:, piece][:, None]).astype(jnp.float32)
            picked = picked * live[None, :, :, None]
            total = total + jnp.einsum("mbsd,bsde->mbe", picked, weight_o[:, piece].astype(jnp.float32), precision=lax.Precision.HIGHEST)
        return total

    summed = lax.map(per_output, (weights, rows_idx, counts))
    summed = jnp.transpose(summed, (1, 0, 2, 3)).reshape(height, NEURONS)
    return jax.nn.relu(summed + shifts[None, :]).astype(jnp.bfloat16)


def reference(features, tiles, tile_rows, tile_counts, bias):
    current = features
    for layer in range(LAYERS):
        current = one_layer(current, tiles[layer], tile_rows[layer], tile_counts[layer], bias[layer])
    return current
```

```python
import functools

import jax
import jax.numpy as jnp
from jax import lax
from jax.experimental import pallas as pl
from jax.experimental.pallas import tpu as pltpu
from jax.sharding import PartitionSpec as P

MESH = pl.DeviceIdType.MESH
PARTS = 4


def partial_products(rows_x, tiles, tile_rows, tile_counts, layer):
    tile_width = tiles.shape[-1]
    out_count = tiles.shape[1] * tiles.shape[2]
    slots = tiles.shape[4]
    height = rows_x.shape[0]
    blocks = rows_x.reshape(height, -1, tile_width)
    picks = tile_rows[layer].reshape(-1)
    picked = jnp.take(blocks, picks, axis=1)
    live = lax.broadcasted_iota(jnp.int32, (out_count, slots), 1) < tile_counts[layer].reshape(
        out_count, 1
    )
    picked = (
        picked.reshape(height, out_count, slots, tile_width)
        * live.astype(jnp.bfloat16)[None, :, :, None]
    )
    weights = tiles[layer].reshape(out_count, slots, tile_width, tile_width)
    summed = jnp.einsum("rosd,osde->roe", picked, weights, preferred_element_type=jnp.float32)
    return summed.reshape(height, out_count * tile_width)


def finish(summed, bias, layer):
    partial_value = lax.psum_scatter(summed, ("col", "rep"), scatter_dimension=1, tiled=True)
    width = partial_value.shape[1]
    offset = lax.axis_index("row") * width
    shifts = lax.dynamic_slice_in_dim(bias[layer], offset, width)
    return jax.nn.relu(partial_value + shifts[None, :]).astype(jnp.bfloat16)


def in_operations(features, tiles, tile_rows, tile_counts, bias):
    layers = tiles.shape[0]
    rows_x = lax.all_gather(features, "row", axis=0, tiled=True)
    for layer in range(layers):
        finished = finish(partial_products(rows_x, tiles, tile_rows, tile_counts, layer), bias, layer)
        if layer + 1 < layers:
            rows_x = lax.all_gather(finished, "row", axis=1, tiled=True)
    return lax.all_to_all(finished, "row", split_axis=0, concat_axis=1, tiled=True)


class Chain:
    def __init__(self, count, place, sems):
        self.count, self.place, self.sems = count, place, sems
        self.me = lax.axis_index("row")

    def copy(self, way, hop, part):
        step = 1 - 2 * way
        shard = jnp.clip(self.me - step * hop, 0, self.count - 1)
        ref = self.place(shard, part)
        return pltpu.make_async_remote_copy(
            src_ref=ref,
            dst_ref=ref,
            send_sem=self.sems.at[0, way, hop, part],
            recv_sem=self.sems.at[1, way, hop, part],
            device_id={"row": jnp.clip(self.me + step, 0, self.count - 1)},
            device_id_type=MESH,
        )

    def sends(self, way, hop):
        if way == 0:
            return (self.me >= hop) & (self.me < self.count - 1)
        return (self.me + hop < self.count) & (self.me > 0)

    def receives(self, way, hop):
        if way == 0:
            return self.me > hop
        return self.me + hop + 1 < self.count

    def start(self, hop, part):
        for way in range(2):

            @pl.when(self.sends(way, hop))
            def _():
                self.copy(way, hop, part).start()

    def wait(self, way, hop, part):
        @pl.when(self.receives(way, hop))
        def _():
            step = 1 - 2 * way
            ref = self.place(jnp.clip(self.me - step * (hop + 1), 0, self.count - 1), part)
            pltpu.make_async_remote_copy(
                src_ref=ref,
                dst_ref=ref,
                send_sem=self.sems.at[0, way, hop, part],
                recv_sem=self.sems.at[1, way, hop, part],
                device_id={"row": jnp.clip(self.me - step, 0, self.count - 1)},
                device_id_type=MESH,
            ).wait_recv()

    def hand_on(self):
        for hop in range(self.count - 1):

            def step(part, carry):
                for way in range(2):
                    self.wait(way, hop, part)
                    if hop + 1 < self.count - 1:

                        @pl.when(self.sends(way, hop + 1))
                        def _():
                            self.copy(way, hop + 1, part).start()

                return carry

            lax.fori_loop(0, PARTS, step, 0)

    def drain(self):
        for hop in range(self.count - 1):

            def step(part, carry):
                for way in range(2):

                    @pl.when(self.sends(way, hop))
                    def _():
                        self.copy(way, hop, part).wait_send()

                return carry

            lax.fori_loop(0, PARTS, step, 0)


def network(
    count, picks_ref, features_ref, tiles_ref, bias_ref, out_ref,
    weights, raw, x_first, x_second, sib_out, sib_in, far_out, far_in, total, turn_out, turn_in,
    weight_sem, gather_sem, spread_sem, sib_sem, far_sem, turn_sem,
):
    layers, pieces, owned, slots, side, _ = weights.shape
    row, col, rep = (lax.axis_index(name) for name in ("row", "col", "rep"))
    height = x_first.shape[1]
    mine = height // count
    pairs = raw.shape[1]
    each = owned // PARTS
    f32, bf16 = jnp.float32, jnp.bfloat16

    def load_weights(layer, piece):
        return pltpu.make_async_copy(
            tiles_ref.at[layer, piece], weights.at[layer, piece], weight_sem.at[layer, piece]
        )

    order = [(1 - col) * 2 + 1 - rep, (1 - col) * 2 + rep, col * 2 + 1 - rep, col * 2 + rep]
    for layer in range(layers):
        for piece in order:
            load_weights(layer, piece).start()

    barrier = pltpu.get_barrier_semaphore()
    for away in range(1, count):
        pl.semaphore_signal(
            barrier, inc=1, device_id={"row": lax.rem(row + away, count)}, device_id_type=MESH
        )
    pl.semaphore_signal(barrier, inc=1, device_id={"rep": 1 - rep}, device_id_type=MESH)
    pl.semaphore_signal(barrier, inc=1, device_id={"col": 1 - col}, device_id_type=MESH)

    def columns(block):
        return pl.ds(pl.multiple_of(block * side, side), side)

    def pack(at, carry):
        low = features_ref[:, columns(at)].astype(f32)
        high = features_ref[:, columns(at + pairs)].astype(f32)
        raw[row, at] = jnp.concatenate([low, high], axis=0).astype(bf16)
        return carry

    lax.fori_loop(0, pairs, pack, 0, unroll=8)
    pl.semaphore_wait(barrier, count + 1)

    share = pairs // PARTS
    gather = Chain(count, lambda shard, part: raw.at[shard, pl.ds(part * share, share)], gather_sem)
    lax.fori_loop(0, PARTS, lambda part, carry: (gather.start(0, part), carry)[1], 0)
    for x in (x_first, x_second):
        x[2 * pairs] = jnp.zeros(x.shape[1:], bf16)
    gather.hand_on()

    def unpack(at, carry):
        slabs = [raw[shard, at].astype(f32) for shard in range(count)]
        x_first[at] = jnp.concatenate([s[:mine] for s in slabs], axis=0).astype(bf16)
        x_first[at + pairs] = jnp.concatenate([s[mine:] for s in slabs], axis=0).astype(bf16)
        return carry

    lax.fori_loop(0, pairs, unpack, 0, unroll=4)

    spread = Chain(
        count, lambda shard, part: x_second.at[pl.ds(shard * owned + part * each, each)], spread_sem
    )

    def sib_copy(layer, which, part):
        at = pl.ds(part * each, each)
        return pltpu.make_async_remote_copy(
            src_ref=sib_out.at[layer, which, at],
            dst_ref=sib_in.at[layer, which, at],
            send_sem=sib_sem.at[0, layer, which, part],
            recv_sem=sib_sem.at[1, layer, which, part],
            device_id={"rep": 1 - rep},
            device_id_type=MESH,
        )

    def far_copy(layer, part):
        at = pl.ds(part * each, each)
        return pltpu.make_async_remote_copy(
            src_ref=far_out.at[layer, at],
            dst_ref=far_in.at[layer, at],
            send_sem=far_sem.at[0, layer, part],
            recv_sem=far_sem.at[1, layer, part],
            device_id={"col": 1 - col},
            device_id_type=MESH,
        )

    def turn_copy(away, part, sender):
        target = lax.rem(row + away, count)
        at = pl.ds(part * (each // 2), each // 2)
        return pltpu.make_async_remote_copy(
            src_ref=turn_out.at[target, at],
            dst_ref=turn_in.at[sender, at],
            send_sem=turn_sem.at[0, away, part],
            recv_sem=turn_sem.at[1, away, part],
            device_id={"row": target},
            device_id_type=MESH,
        )

    for layer in range(layers):
        x = x_first if layer == 0 else x_second

        def product(piece, block):
            first = ((layer * pieces + piece) * owned + block) * slots
            picked = [x[picks_ref[first + slot]] for slot in range(slots)]
            tile = weights[layer, piece, block].reshape(slots * side, side)
            return jnp.dot(jnp.concatenate(picked, axis=1), tile, preferred_element_type=f32)

        def for_sibling(which, piece):
            load_weights(layer, piece).wait()

            def step(part, carry):
                for k in range(each):
                    block = part * each + k
                    sib_out[layer, which, block] = product(piece, block).astype(bf16)
                sib_copy(layer, which, part).start()
                return carry

            lax.fori_loop(0, PARTS, step, 0)

        for_sibling(0, order[0])
        load_weights(layer, order[1]).wait()

        def for_far(part, carry):
            sib_copy(layer, 0, part).wait_recv()
            for k in range(each):
                block = part * each + k
                value = product(order[1], block) + sib_in[layer, 0, block].astype(f32)
                far_out[layer, block] = value.astype(bf16)
            far_copy(layer, part).start()
            return carry

        lax.fori_loop(0, PARTS, for_far, 0)
        for_sibling(1, order[2])
        load_weights(layer, order[3]).wait()

        def own(part, carry):
            sib_copy(layer, 1, part).wait_recv()
            for k in range(each):
                block = part * each + k
                total[block] = product(order[3], block) + sib_in[layer, 1, block].astype(f32)
            return carry

        lax.fori_loop(0, PARTS, own, 0)

        def done(block):
            shift = bias_ref[layer : layer + 1, columns(row * owned + block)]
            value = total[block] + far_in[layer, block].astype(f32) + shift
            return jnp.maximum(value, 0.0)

        def close(part, carry):
            far_copy(layer, part).wait_recv()
            if layer + 1 < layers:
                for k in range(each):
                    block = part * each + k
                    x_second[row * owned + block] = done(block).astype(bf16)
                spread.start(0, part)
            else:
                half = each // 2
                for k in range(half):
                    at = part * half + k
                    low, high = done(part * each + k), done(part * each + half + k)
                    for target in range(count):
                        rows = slice(target * mine, (target + 1) * mine)
                        slab = jnp.concatenate([low[rows], high[rows]], axis=0).astype(bf16)
                        turn_out[target, at] = slab
                for away in range(1, count):
                    turn_copy(away, part, row).start()
            return carry

        lax.fori_loop(0, PARTS, close, 0)
        if layer + 1 < layers:
            spread.hand_on()

    def put(sender, source, index, at):
        half = each // 2
        slab = source[index, at].astype(f32)
        block = sender * owned + (at // half) * each + at % half
        out_ref[:, columns(block)] = slab[:mine].astype(bf16)
        out_ref[:, columns(block + half)] = slab[mine:].astype(bf16)

    def put_all(sender, source, index):
        def step(at, carry):
            put(sender, source, index, at)
            return carry

        lax.fori_loop(0, owned // 2, step, 0, unroll=4)

    put_all(row, turn_out, row)
    for away in range(1, count):
        sender = lax.rem(row + count - away, count)
        lax.fori_loop(
            0, PARTS, lambda part, carry: (turn_copy(away, part, sender).wait_recv(), carry)[1], 0
        )
        put_all(sender, turn_in, sender)

    def settle(part, carry):
        for layer in range(layers):
            far_copy(layer, part).wait_send()
            for which in range(2):
                sib_copy(layer, which, part).wait_send()
        for away in range(1, count):
            turn_copy(away, part, row).wait_send()
        return carry

    lax.fori_loop(0, PARTS, settle, 0)
    gather.drain()
    spread.drain()


def in_kernel(count, features, tiles, tile_rows, tile_counts, bias):
    layers, pieces, owned, _, slots, side, _ = tiles.shape
    mine, width = features.shape
    blocks = width // side
    height = mine * count
    live = lax.broadcasted_iota(jnp.int32, tile_rows.shape, 4) < tile_counts[..., None]
    picks = jnp.where(live, tile_rows, blocks).reshape(-1)
    bf16, dma = jnp.bfloat16, pltpu.SemaphoreType.DMA
    return pl.pallas_call(
        functools.partial(network, count),
        out_shape=jax.ShapeDtypeStruct((mine, width), bf16),
        in_specs=[
            pl.BlockSpec(memory_space=pltpu.SMEM),
            pl.BlockSpec(memory_space=pltpu.VMEM),
            pl.BlockSpec(memory_space=pl.ANY),
            pl.BlockSpec(memory_space=pltpu.VMEM),
        ],
        out_specs=pl.BlockSpec(memory_space=pltpu.VMEM),
        scratch_shapes=[
            pltpu.VMEM((layers, pieces, owned, slots, side, side), bf16),
            pltpu.VMEM((count, blocks // 2, 2 * mine, side), bf16),
            pltpu.VMEM((blocks + 1, height, side), bf16),
            pltpu.VMEM((blocks + 1, height, side), bf16),
            pltpu.VMEM((layers, 2, owned, height, side), bf16),
            pltpu.VMEM((layers, 2, owned, height, side), bf16),
            pltpu.VMEM((layers, owned, height, side), bf16),
            pltpu.VMEM((layers, owned, height, side), bf16),
            pltpu.VMEM((owned, height, side), jnp.float32),
            pltpu.VMEM((count, owned // 2, 2 * mine, side), bf16),
            pltpu.VMEM((count, owned // 2, 2 * mine, side), bf16),
            dma((layers, pieces)),
            dma((2, 2, count - 1, PARTS)),
            dma((2, 2, count - 1, PARTS)),
            dma((2, layers, 2, PARTS)),
            dma((2, layers, PARTS)),
            dma((2, count, PARTS)),
        ],
        compiler_params=pltpu.CompilerParams(
            collective_id=0, has_side_effects=True, vmem_limit_bytes=48 * 2**20
        ),
        name="network",
    )(picks, features, tiles.reshape(layers, pieces, owned, slots, side, side), bias)


def on_device(sizes, features, tiles, tile_rows, tile_counts, bias):
    count = sizes["row"]
    owned = tiles.shape[2]
    fits = (
        tiles.shape[0] == 2
        and sizes["col"] == 2
        and sizes["rep"] == 2
        and 1 < count <= 4
        and features.shape[0] == 8
        and owned % (2 * PARTS) == 0
        and 2 * tiles[0].size * 2 <= 32 * 2**20
    )
    body = functools.partial(in_kernel, count) if fits else in_operations
    return body(features, tiles, tile_rows, tile_counts, bias)


def solution(mesh):
    in_specs = (
        P(("grp", "row"), ("col", "rep")),
        P(None, None, "row", ("col", "rep"), None, None, None),
        P(None, None, "row", ("col", "rep"), None),
        P(None, None, "row", ("col", "rep")),
        P(None, ("col", "rep")),
    )
    out_specs = P(("grp", "row"), ("col", "rep"))
    return jax.shard_map(
        functools.partial(on_device, dict(mesh.shape)),
        mesh=mesh, in_specs=in_specs, out_specs=out_specs, check_vma=False,
    )
```

```python
import functools

import jax
import jax.numpy as jnp
from jax import lax
from jax.experimental import pallas as pl
from jax.experimental.pallas import tpu as pltpu
from jax.sharding import PartitionSpec as P

MESH = pl.DeviceIdType.MESH
PARTS = 4
CHUNKS = 2


def partial_products(rows_x, tiles, tile_rows, tile_counts, layer):
    tile_width = tiles.shape[-1]
    out_count = tiles.shape[1] * tiles.shape[2]
    slots = tiles.shape[4]
    height = rows_x.shape[0]
    blocks = rows_x.reshape(height, -1, tile_width)
    picks = tile_rows[layer].reshape(-1)
    picked = jnp.take(blocks, picks, axis=1)
    live = lax.broadcasted_iota(jnp.int32, (out_count, slots), 1) < tile_counts[layer].reshape(
        out_count, 1
    )
    picked = (
        picked.reshape(height, out_count, slots, tile_width)
        * live.astype(jnp.bfloat16)[None, :, :, None]
    )
    weights = tiles[layer].reshape(out_count, slots, tile_width, tile_width)
    summed = jnp.einsum("rosd,osde->roe", picked, weights, preferred_element_type=jnp.float32)
    return summed.reshape(height, out_count * tile_width)


def finish(summed, bias, layer):
    partial_value = lax.psum_scatter(summed, ("col", "rep"), scatter_dimension=1, tiled=True)
    width = partial_value.shape[1]
    offset = lax.axis_index("row") * width
    shifts = lax.dynamic_slice_in_dim(bias[layer], offset, width)
    return jax.nn.relu(partial_value + shifts[None, :]).astype(jnp.bfloat16)


def in_operations(features, tiles, tile_rows, tile_counts, bias):
    layers = tiles.shape[0]
    rows_x = lax.all_gather(features, "row", axis=0, tiled=True)
    for layer in range(layers):
        finished = finish(partial_products(rows_x, tiles, tile_rows, tile_counts, layer), bias, layer)
        if layer + 1 < layers:
            rows_x = lax.all_gather(finished, "row", axis=1, tiled=True)
    return lax.all_to_all(finished, "row", split_axis=0, concat_axis=1, tiled=True)


class Line:
    MOVES = ((2, 2), (3, -2), (0, 1), (1, -1))
    ON = 4

    def __init__(self, count, place, sems):
        self.count, self.place, self.sems = count, place, sems
        self.me = lax.axis_index("row")

    def copy(self, slot, step, shard, part):
        ref = self.place(jnp.clip(shard, 0, self.count - 1), part)
        return pltpu.make_async_remote_copy(
            src_ref=ref,
            dst_ref=ref,
            send_sem=self.sems.at[0, slot, part],
            recv_sem=self.sems.at[1, slot, part],
            device_id={"row": jnp.clip(self.me + step, 0, self.count - 1)},
            device_id_type=MESH,
        )

    def inside(self, step):
        return self.me < self.count - step if step > 0 else self.me >= -step

    def start(self, part):
        for slot, step in self.MOVES:

            @pl.when(self.inside(step))
            def _():
                self.copy(slot, step, self.me, part).start()

    def hand_on(self, part):
        for place, slot, step, shard in ((1, 3, -1, 3), (2, 2, 1, 0)):

            @pl.when(self.me == place)
            def _():
                self.copy(slot, step, shard, part).wait_recv()
                self.copy(self.ON, step, shard, part).start()

    def wait(self, part):
        for slot, step in self.MOVES:
            came = self.inside(-step)
            if abs(step) == 2:
                came = came & ((self.me == 0) | (self.me == self.count - 1))

            @pl.when(came)
            def _():
                back = 1 if step < 0 else -1
                self.copy(slot, back, self.me - step, part).wait_recv()

        for place, step, shard in ((0, 1, 3), (3, -1, 0)):

            @pl.when(self.me == place)
            def _():
                self.copy(self.ON, step, shard, part).wait_recv()

    def drain(self, part):
        for slot, step in self.MOVES:

            @pl.when(self.inside(step))
            def _():
                self.copy(slot, step, self.me, part).wait_send()

        for place, step, shard in ((1, -1, 3), (2, 1, 0)):

            @pl.when(self.me == place)
            def _():
                self.copy(self.ON, step, shard, part).wait_send()


def each_part(body):
    def step(part, carry):
        body(part)
        return carry

    lax.fori_loop(0, PARTS, step, 0)


def network(
    count, picks_ref, features_ref, tiles_ref, bias_ref, out_ref,
    weights, given, shifts, raw, x_first, x_second_low, x_second_high, sib_out, sib_in, far_out, far_in, total, turn_out, turn_in,
    weight_sem, load_sem, gather_sem, spread_sem, sib_sem, far_sem, turn_sem,
):
    layers, pieces, owned, slots, side, _ = weights.shape
    row, col, rep = (lax.axis_index(name) for name in ("row", "col", "rep"))
    chunks, slabs, height = raw.shape[0], raw.shape[2], raw.shape[3]
    piece_rows = height // count
    stack = height // piece_rows
    each = owned // PARTS
    f32, bf16 = jnp.float32, jnp.bfloat16

    x_second = (x_second_low, x_second_high)
    take_features = pltpu.make_async_copy(features_ref, given, load_sem.at[0])
    take_bias = pltpu.make_async_copy(bias_ref, shifts, load_sem.at[1])
    take_features.start()

    def load_weights(layer, piece):
        return pltpu.make_async_copy(
            tiles_ref.at[layer, piece], weights.at[layer, piece], weight_sem.at[layer, piece]
        )

    barrier = pltpu.get_barrier_semaphore()
    for away in range(1, count):
        pl.semaphore_signal(
            barrier, inc=1, device_id={"row": lax.rem(row + away, count)}, device_id_type=MESH
        )
    pl.semaphore_signal(barrier, inc=1, device_id={"rep": 1 - rep}, device_id_type=MESH)
    pl.semaphore_signal(barrier, inc=1, device_id={"col": 1 - col}, device_id_type=MESH)

    order = [(1 - col) * 2 + 1 - rep, (1 - col) * 2 + rep, col * 2 + 1 - rep, col * 2 + rep]
    take_features.wait()
    for layer in range(layers):
        for piece in order:
            load_weights(layer, piece).start()
    take_bias.start()

    def columns(block):
        return pl.ds(pl.multiple_of(block * side, side), side)

    def pack(at, carry):
        values = [given[:, columns(at + j * slabs)].astype(f32) for j in range(stack)]
        for chunk in range(chunks):
            rows = slice(chunk * piece_rows, (chunk + 1) * piece_rows)
            raw[chunk, row, at] = jnp.concatenate([v[rows] for v in values], axis=0).astype(bf16)
        return carry

    lax.fori_loop(0, slabs, pack, 0, unroll=4)
    pl.semaphore_wait(barrier, count + 1)

    share = slabs // PARTS
    gathers, spreads = [], []
    for chunk in range(chunks):

        def raw_place(shard, part, chunk=chunk):
            return raw.at[chunk, shard, pl.ds(part * share, share)]

        def second_place(shard, part, chunk=chunk):
            return x_second[chunk].at[pl.ds(shard * owned + part * each, each)]

        gathers.append(Line(count, raw_place, gather_sem.at[chunk]))
        spreads.append(Line(count, second_place, spread_sem.at[chunk]))
    for chunk in range(chunks):
        each_part(gathers[chunk].start)
    for chunk in range(chunks):
        for x in (x_first.at[chunk], x_second[chunk]):
            x[stack * slabs] = jnp.zeros(x.shape[1:], bf16)

    def unpack(chunk):
        def step(at, carry):
            values = [raw[chunk, shard, at].astype(f32) for shard in range(count)]
            for j in range(stack):
                rows = slice(j * piece_rows, (j + 1) * piece_rows)
                block = jnp.concatenate([v[rows] for v in values], axis=0).astype(bf16)
                x_first[chunk, at + j * slabs] = block
            return carry

        lax.fori_loop(0, slabs, step, 0, unroll=4)

    def sib_copy(layer, chunk, which, part):
        at = pl.ds(part * each, each)
        return pltpu.make_async_remote_copy(
            src_ref=sib_out.at[layer, chunk, which, at],
            dst_ref=sib_in.at[layer, chunk, which, at],
            send_sem=sib_sem.at[0, layer, chunk, which, part],
            recv_sem=sib_sem.at[1, layer, chunk, which, part],
            device_id={"rep": 1 - rep},
            device_id_type=MESH,
        )

    def far_copy(layer, chunk, part):
        at = pl.ds(part * each, each)
        return pltpu.make_async_remote_copy(
            src_ref=far_out.at[layer, chunk, at],
            dst_ref=far_in.at[layer, chunk, at],
            send_sem=far_sem.at[0, layer, chunk, part],
            recv_sem=far_sem.at[1, layer, chunk, part],
            device_id={"col": 1 - col},
            device_id_type=MESH,
        )

    per_part = each // stack

    def turn_copy(chunk, away, part, sender):
        target = lax.rem(row + away, count)
        at = pl.ds(part * per_part, per_part)
        return pltpu.make_async_remote_copy(
            src_ref=turn_out.at[chunk, target, at],
            dst_ref=turn_in.at[chunk, sender, at],
            send_sem=turn_sem.at[0, chunk, away, part],
            recv_sem=turn_sem.at[1, chunk, away, part],
            device_id={"row": target},
            device_id_type=MESH,
        )

    def run(layer, chunk, beside):
        x = x_first.at[chunk] if layer == 0 else x_second[chunk]

        def ready(piece):
            if chunk == 0:
                load_weights(layer, piece).wait()

        def product(piece, block):
            first = ((layer * pieces + piece) * owned + block) * slots
            picked = [x[picks_ref[first + slot]] for slot in range(slots)]
            tile = weights[layer, piece, block].reshape(slots * side, side)
            return jnp.dot(jnp.concatenate(picked, axis=1), tile, preferred_element_type=f32)

        def for_sibling(which, piece):
            ready(piece)

            def step(part):
                for k in range(each):
                    block = part * each + k
                    sib_out[layer, chunk, which, block] = product(piece, block)
                sib_copy(layer, chunk, which, part).start()
                if which == 1 and beside is not None:
                    beside.hand_on(part)

            each_part(step)

        for_sibling(0, order[0])
        ready(order[1])

        def for_far(part):
            sib_copy(layer, chunk, 0, part).wait_recv()
            for k in range(each):
                block = part * each + k
                value = product(order[1], block) + sib_in[layer, chunk, 0, block]
                far_out[layer, chunk, block] = value.astype(bf16)
            far_copy(layer, chunk, part).start()

        each_part(for_far)
        for_sibling(1, order[2])
        ready(order[3])

        def own(part):
            sib_copy(layer, chunk, 1, part).wait_recv()
            for k in range(each):
                block = part * each + k
                total[block] = product(order[3], block) + sib_in[layer, chunk, 1, block]

        each_part(own)

        def done(block):
            shift = shifts[layer : layer + 1, columns(row * owned + block)]
            value = total[block] + far_in[layer, chunk, block].astype(f32) + shift
            return jnp.maximum(value, 0.0)

        def close(part):
            far_copy(layer, chunk, part).wait_recv()
            if layer + 1 < layers:
                for k in range(each):
                    block = part * each + k
                    x_second[chunk][row * owned + block] = done(block).astype(bf16)
                spreads[chunk].start(part)
            else:
                for k in range(per_part):
                    at = part * per_part + k
                    values = [done(part * each + j * per_part + k) for j in range(stack)]
                    for target in range(count):
                        rows = slice(target * piece_rows, (target + 1) * piece_rows)
                        slab = jnp.concatenate([v[rows] for v in values], axis=0).astype(bf16)
                        turn_out[chunk, target, at] = slab
                for away in range(1, count):
                    turn_copy(chunk, away, part, row).start()

        each_part(close)

    each_part(gathers[0].hand_on)
    each_part(gathers[0].wait)
    unpack(0)
    take_bias.wait()
    run(0, 0, gathers[1])
    each_part(gathers[1].wait)
    unpack(1)
    run(0, 1, spreads[0])
    each_part(spreads[0].wait)
    run(1, 0, spreads[1])
    each_part(spreads[1].wait)
    run(1, 1, None)

    def put_all(sender, source, index):
        def step(at, carry):
            values = [source[chunk, index, at].astype(f32) for chunk in range(chunks)]
            for j in range(stack):
                rows = slice(j * piece_rows, (j + 1) * piece_rows)
                block = sender * owned + (at // per_part) * each + j * per_part + at % per_part
                both = jnp.concatenate([v[rows] for v in values], axis=0)
                out_ref[:, columns(block)] = both.astype(bf16)
            return carry

        lax.fori_loop(0, owned // stack, step, 0, unroll=4)

    put_all(row, turn_out, row)
    for away in range(1, count):
        sender = lax.rem(row + count - away, count)
        for chunk in range(chunks):
            each_part(lambda part: turn_copy(chunk, away, part, sender).wait_recv())
        put_all(sender, turn_in, sender)

    def settle(part):
        for chunk in range(chunks):
            for layer in range(layers):
                far_copy(layer, chunk, part).wait_send()
                for which in range(2):
                    sib_copy(layer, chunk, which, part).wait_send()
            for away in range(1, count):
                turn_copy(chunk, away, part, row).wait_send()
            gathers[chunk].drain(part)
            spreads[chunk].drain(part)

    each_part(settle)


def in_kernel(count, features, tiles, tile_rows, tile_counts, bias):
    layers, pieces, owned, _, slots, side, _ = tiles.shape
    mine, width = features.shape
    blocks = width // side
    height = mine * count // CHUNKS
    stack = count
    live = lax.broadcasted_iota(jnp.int32, tile_rows.shape, 4) < tile_counts[..., None]
    picks = jnp.where(live, tile_rows, blocks).reshape(-1)
    f32, bf16, dma = jnp.float32, jnp.bfloat16, pltpu.SemaphoreType.DMA
    turned = (CHUNKS, count, owned // stack, height, side)
    return pl.pallas_call(
        functools.partial(network, count),
        out_shape=jax.ShapeDtypeStruct((mine, width), bf16),
        in_specs=[
            pl.BlockSpec(memory_space=pltpu.SMEM),
            pl.BlockSpec(memory_space=pl.ANY),
            pl.BlockSpec(memory_space=pl.ANY),
            pl.BlockSpec(memory_space=pl.ANY),
        ],
        out_specs=pl.BlockSpec(memory_space=pltpu.VMEM),
        scratch_shapes=[
            pltpu.VMEM((layers, pieces, owned, slots, side, side), bf16),
            pltpu.VMEM((mine, width), bf16),
            pltpu.VMEM(bias.shape, f32),
            pltpu.VMEM((CHUNKS, count, blocks // stack, height, side), bf16),
            pltpu.VMEM((CHUNKS, blocks + 1, height, side), bf16),
            pltpu.VMEM((blocks + 1, height, side), bf16),
            pltpu.VMEM((blocks + 1, height, side), bf16),
            pltpu.VMEM((layers, CHUNKS, 2, owned, height, side), f32),
            pltpu.VMEM((layers, CHUNKS, 2, owned, height, side), f32),
            pltpu.VMEM((layers, CHUNKS, owned, height, side), bf16),
            pltpu.VMEM((layers, CHUNKS, owned, height, side), bf16),
            pltpu.VMEM((owned, height, side), f32),
            pltpu.VMEM(turned, bf16),
            pltpu.VMEM(turned, bf16),
            dma((layers, pieces)),
            dma((2,)),
            dma((CHUNKS, 2, 5, PARTS)),
            dma((CHUNKS, 2, 5, PARTS)),
            dma((2, layers, CHUNKS, 2, PARTS)),
            dma((2, layers, CHUNKS, PARTS)),
            dma((2, CHUNKS, count, PARTS)),
        ],
        compiler_params=pltpu.CompilerParams(
            collective_id=0, has_side_effects=True, vmem_limit_bytes=56 * 2**20
        ),
        name="network",
    )(picks, features, tiles.reshape(layers, pieces, owned, slots, side, side), bias)


def on_device(sizes, features, tiles, tile_rows, tile_counts, bias):
    count = sizes["row"]
    owned = tiles.shape[2]
    fits = (
        tiles.shape[0] == 2
        and sizes["col"] == 2
        and sizes["rep"] == 2
        and count == 4
        and features.shape[0] == 8
        and owned % (4 * PARTS) == 0
        and 2 * tiles[0].size * 2 <= 32 * 2**20
    )
    body = functools.partial(in_kernel, count) if fits else in_operations
    return body(features, tiles, tile_rows, tile_counts, bias)


def solution(mesh):
    in_specs = (
        P(("grp", "row"), ("col", "rep")),
        P(None, None, "row", ("col", "rep"), None, None, None),
        P(None, None, "row", ("col", "rep"), None),
        P(None, None, "row", ("col", "rep")),
        P(None, ("col", "rep")),
    )
    out_specs = P(("grp", "row"), ("col", "rep"))
    return jax.shard_map(
        functools.partial(on_device, dict(mesh.shape)),
        mesh=mesh, in_specs=in_specs, out_specs=out_specs, check_vma=False,
    )
```

```python
import functools

import jax
import jax.numpy as jnp
from jax import lax
from jax.experimental import pallas as pl
from jax.experimental.pallas import tpu as pltpu
from jax.sharding import PartitionSpec as P

MESH = pl.DeviceIdType.MESH
PARTS = 4
CHUNKS = 2


def partial_products(rows_x, tiles, tile_rows, tile_counts, layer):
    tile_width = tiles.shape[-1]
    out_count = tiles.shape[1] * tiles.shape[2]
    slots = tiles.shape[4]
    height = rows_x.shape[0]
    blocks = rows_x.reshape(height, -1, tile_width)
    picks = tile_rows[layer].reshape(-1)
    picked = jnp.take(blocks, picks, axis=1)
    live = lax.broadcasted_iota(jnp.int32, (out_count, slots), 1) < tile_counts[layer].reshape(
        out_count, 1
    )
    picked = (
        picked.reshape(height, out_count, slots, tile_width)
        * live.astype(jnp.bfloat16)[None, :, :, None]
    )
    weights = tiles[layer].reshape(out_count, slots, tile_width, tile_width)
    summed = jnp.einsum("rosd,osde->roe", picked, weights, preferred_element_type=jnp.float32)
    return summed.reshape(height, out_count * tile_width)


def finish(summed, bias, layer):
    partial_value = lax.psum_scatter(summed, ("col", "rep"), scatter_dimension=1, tiled=True)
    width = partial_value.shape[1]
    offset = lax.axis_index("row") * width
    shifts = lax.dynamic_slice_in_dim(bias[layer], offset, width)
    return jax.nn.relu(partial_value + shifts[None, :]).astype(jnp.bfloat16)


def in_operations(features, tiles, tile_rows, tile_counts, bias):
    layers = tiles.shape[0]
    rows_x = lax.all_gather(features, "row", axis=0, tiled=True)
    for layer in range(layers):
        finished = finish(partial_products(rows_x, tiles, tile_rows, tile_counts, layer), bias, layer)
        if layer + 1 < layers:
            rows_x = lax.all_gather(finished, "row", axis=1, tiled=True)
    return lax.all_to_all(finished, "row", split_axis=0, concat_axis=1, tiled=True)


class Line:
    MOVES = ((2, 2), (3, -2), (0, 1), (1, -1))
    ON = 4

    def __init__(self, count, place, sems):
        self.count, self.place, self.sems = count, place, sems
        self.me = lax.axis_index("row")

    def copy(self, slot, step, shard, part):
        ref = self.place(jnp.clip(shard, 0, self.count - 1), part)
        own = part if slot in (2, 3) and part is not None else 0
        return pltpu.make_async_remote_copy(
            src_ref=ref,
            dst_ref=ref,
            send_sem=self.sems.at[0, slot, 0],
            recv_sem=self.sems.at[1, slot, own],
            device_id={"row": jnp.clip(self.me + step, 0, self.count - 1)},
            device_id_type=MESH,
        )

    def inside(self, step):
        return self.me < self.count - step if step > 0 else self.me >= -step

    def start(self, part):
        for slot, step in self.MOVES:

            @pl.when(self.inside(step))
            def _():
                self.copy(slot, step, self.me, part).start()

    def hand_on(self, part):
        for place, slot, step, shard in ((1, 3, -1, 3), (2, 2, 1, 0)):

            @pl.when(self.me == place)
            def _():
                self.copy(slot, step, shard, part).wait_recv()
                self.copy(self.ON, step, shard, part).start()

    def wait(self):
        for slot, step in self.MOVES:
            came = self.inside(-step)
            if abs(step) == 2:
                came = came & ((self.me == 0) | (self.me == self.count - 1))

            @pl.when(came)
            def _():
                back = 1 if step < 0 else -1
                if abs(step) == 2:
                    each_part(lambda part: self.copy(slot, back, self.me - step, part).wait_recv())
                else:
                    self.copy(slot, back, self.me - step, None).wait_recv()

        for place, step, shard in ((0, 1, 3), (3, -1, 0)):

            @pl.when(self.me == place)
            def _():
                self.copy(self.ON, step, shard, None).wait_recv()

    def drain(self):
        for slot, step in self.MOVES:

            @pl.when(self.inside(step))
            def _():
                self.copy(slot, step, self.me, None).wait_send()

        for place, step, shard in ((1, -1, 3), (2, 1, 0)):

            @pl.when(self.me == place)
            def _():
                self.copy(self.ON, step, shard, None).wait_send()


def each_part(body):
    def step(part, carry):
        body(part)
        return carry

    lax.fori_loop(0, PARTS, step, 0)


def network(
    count, picks_ref, features_ref, tiles_ref, bias_ref, out_ref,
    weights, given, shifts, raw, x_first, x_second_low, x_second_high, sib_out, sib_in, far_out, far_in, total, turn_out, turn_in,
    weight_sem, load_sem, gather_sem, spread_sem, sib_sem, far_sem, turn_sem,
):
    layers, pieces, owned, slots, side, _ = weights.shape
    row, col, rep = (lax.axis_index(name) for name in ("row", "col", "rep"))
    chunks, slabs, height = raw.shape[0], raw.shape[2], raw.shape[3]
    piece_rows = height // count
    stack = height // piece_rows
    each = owned // PARTS
    f32, bf16 = jnp.float32, jnp.bfloat16

    x_second = (x_second_low, x_second_high)
    take_features = pltpu.make_async_copy(features_ref, given, load_sem.at[0])
    take_bias = pltpu.make_async_copy(bias_ref, shifts, load_sem.at[1])
    take_features.start()

    def load_weights(layer, piece):
        return pltpu.make_async_copy(
            tiles_ref.at[layer, piece], weights.at[layer, piece], weight_sem.at[layer, piece]
        )

    barrier = pltpu.get_barrier_semaphore()
    for away in range(1, count):
        pl.semaphore_signal(
            barrier, inc=1, device_id={"row": lax.rem(row + away, count)}, device_id_type=MESH
        )
    pl.semaphore_signal(barrier, inc=1, device_id={"rep": 1 - rep}, device_id_type=MESH)
    pl.semaphore_signal(barrier, inc=1, device_id={"col": 1 - col}, device_id_type=MESH)

    order = [(1 - col) * 2 + 1 - rep, (1 - col) * 2 + rep, col * 2 + 1 - rep, col * 2 + rep]
    take_features.wait()
    for layer in range(layers):
        for piece in order:
            load_weights(layer, piece).start()
    take_bias.start()

    def columns(block):
        return pl.ds(pl.multiple_of(block * side, side), side)

    def pack(at, carry):
        values = [given[:, columns(at + j * slabs)].astype(f32) for j in range(stack)]
        for chunk in range(chunks):
            rows = slice(chunk * piece_rows, (chunk + 1) * piece_rows)
            raw[chunk, row, at] = jnp.concatenate([v[rows] for v in values], axis=0).astype(bf16)
        return carry

    lax.fori_loop(0, slabs, pack, 0, unroll=4)
    pl.semaphore_wait(barrier, count + 1)

    def some(part, size, whole, base=0):
        return pl.ds(base, whole) if part is None else pl.ds(base + part * size, size)

    share = slabs // PARTS
    gathers, spreads = [], []
    for chunk in range(chunks):

        def raw_place(shard, part, chunk=chunk):
            return raw.at[chunk, shard, some(part, share, slabs)]

        def second_place(shard, part, chunk=chunk):
            return x_second[chunk].at[some(part, each, owned, shard * owned)]

        gathers.append(Line(count, raw_place, gather_sem.at[chunk]))
        spreads.append(Line(count, second_place, spread_sem.at[chunk]))
    for chunk in range(chunks):
        each_part(gathers[chunk].start)
    for chunk in range(chunks):
        for x in (x_first.at[chunk], x_second[chunk]):
            x[stack * slabs] = jnp.zeros(x.shape[1:], bf16)

    def unpack(chunk):
        def step(at, carry):
            values = [raw[chunk, shard, at].astype(f32) for shard in range(count)]
            for j in range(stack):
                rows = slice(j * piece_rows, (j + 1) * piece_rows)
                block = jnp.concatenate([v[rows] for v in values], axis=0).astype(bf16)
                x_first[chunk, at + j * slabs] = block
            return carry

        lax.fori_loop(0, slabs, step, 0, unroll=4)

    def sib_copy(layer, chunk, which, part):
        at = some(part, each, owned)
        return pltpu.make_async_remote_copy(
            src_ref=sib_out.at[layer, chunk, which, at],
            dst_ref=sib_in.at[layer, chunk, which, at],
            send_sem=sib_sem.at[0, layer, chunk, which, 0],
            recv_sem=sib_sem.at[1, layer, chunk, which, 0 if part is None else part],
            device_id={"rep": 1 - rep},
            device_id_type=MESH,
        )

    def far_copy(layer, chunk, part):
        at = some(part, each, owned)
        return pltpu.make_async_remote_copy(
            src_ref=far_out.at[layer, chunk, at],
            dst_ref=far_in.at[layer, chunk, at],
            send_sem=far_sem.at[0, layer, chunk, 0],
            recv_sem=far_sem.at[1, layer, chunk, 0 if part is None else part],
            device_id={"col": 1 - col},
            device_id_type=MESH,
        )

    per_part = each // stack

    def turn_copy(chunk, away, part, sender):
        target = lax.rem(row + away, count)
        at = some(part, per_part, owned // stack)
        return pltpu.make_async_remote_copy(
            src_ref=turn_out.at[chunk, target, at],
            dst_ref=turn_in.at[chunk, sender, at],
            send_sem=turn_sem.at[0, chunk, away],
            recv_sem=turn_sem.at[1, chunk, away],
            device_id={"row": target},
            device_id_type=MESH,
        )

    def run(layer, chunk, beside):
        x = x_first.at[chunk] if layer == 0 else x_second[chunk]

        def ready(piece):
            if chunk == 0:
                load_weights(layer, piece).wait()

        def product(piece, block):
            first = ((layer * pieces + piece) * owned + block) * slots
            picked = [x[picks_ref[first + slot]] for slot in range(slots)]
            tile = weights[layer, piece, block].reshape(slots * side, side)
            return jnp.dot(jnp.concatenate(picked, axis=1), tile, preferred_element_type=f32)

        def for_sibling(which, piece):
            ready(piece)

            def step(part):
                for k in range(each):
                    block = part * each + k
                    sib_out[layer, chunk, which, block] = product(piece, block)
                sib_copy(layer, chunk, which, part).start()
                if which == 1 and beside is not None:
                    beside.hand_on(part)

            each_part(step)

        for_sibling(0, order[0])
        ready(order[1])

        def for_far(part):
            sib_copy(layer, chunk, 0, part).wait_recv()
            for k in range(each):
                block = part * each + k
                value = product(order[1], block) + sib_in[layer, chunk, 0, block]
                far_out[layer, chunk, block] = value.astype(bf16)
            far_copy(layer, chunk, part).start()

        each_part(for_far)
        for_sibling(1, order[2])
        ready(order[3])

        def own(part):
            sib_copy(layer, chunk, 1, part).wait_recv()
            for k in range(each):
                block = part * each + k
                total[block] = product(order[3], block) + sib_in[layer, chunk, 1, block]

        each_part(own)

        def done(block):
            shift = shifts[layer : layer + 1, columns(row * owned + block)]
            value = total[block] + far_in[layer, chunk, block].astype(f32) + shift
            return jnp.maximum(value, 0.0)

        def close(part):
            far_copy(layer, chunk, part).wait_recv()
            if layer + 1 < layers:
                for k in range(each):
                    block = part * each + k
                    x_second[chunk][row * owned + block] = done(block).astype(bf16)
                spreads[chunk].start(part)
            else:
                for k in range(per_part):
                    at = part * per_part + k
                    values = [done(part * each + j * per_part + k) for j in range(stack)]
                    for target in range(count):
                        rows = slice(target * piece_rows, (target + 1) * piece_rows)
                        slab = jnp.concatenate([v[rows] for v in values], axis=0).astype(bf16)
                        turn_out[chunk, target, at] = slab
                for away in range(1, count):
                    turn_copy(chunk, away, part, row).start()

        each_part(close)

    def settle(layer, chunk):
        far_copy(layer, chunk, None).wait_send()
        for which in range(2):
            sib_copy(layer, chunk, which, None).wait_send()
        if layer + 1 == layers:
            for away in range(1, count):
                turn_copy(chunk, away, None, row).wait_send()

    each_part(gathers[0].hand_on)
    gathers[0].wait()
    unpack(0)
    take_bias.wait()
    run(0, 0, gathers[1])
    gathers[1].wait()
    unpack(1)
    run(0, 1, spreads[0])
    spreads[0].wait()
    run(1, 0, spreads[1])
    for chunk in range(chunks):
        gathers[chunk].drain()
        settle(0, chunk)
    settle(1, 0)
    spreads[0].drain()
    spreads[1].wait()
    run(1, 1, None)
    spreads[1].drain()

    def put_all(sender, source, index):
        def step(at, carry):
            values = [source[chunk, index, at].astype(f32) for chunk in range(chunks)]
            for j in range(stack):
                rows = slice(j * piece_rows, (j + 1) * piece_rows)
                block = sender * owned + (at // per_part) * each + j * per_part + at % per_part
                both = jnp.concatenate([v[rows] for v in values], axis=0)
                out_ref[:, columns(block)] = both.astype(bf16)
            return carry

        lax.fori_loop(0, owned // stack, step, 0, unroll=4)

    put_all(row, turn_out, row)
    for away in range(1, count):
        sender = lax.rem(row + count - away, count)
        for chunk in range(chunks):
            turn_copy(chunk, away, None, sender).wait_recv()
        put_all(sender, turn_in, sender)
    settle(1, 1)


def in_kernel(count, features, tiles, tile_rows, tile_counts, bias):
    layers, pieces, owned, _, slots, side, _ = tiles.shape
    mine, width = features.shape
    blocks = width // side
    height = mine * count // CHUNKS
    stack = count
    live = lax.broadcasted_iota(jnp.int32, tile_rows.shape, 4) < tile_counts[..., None]
    picks = jnp.where(live, tile_rows, blocks).reshape(-1)
    f32, bf16, dma = jnp.float32, jnp.bfloat16, pltpu.SemaphoreType.DMA
    turned = (CHUNKS, count, owned // stack, height, side)
    return pl.pallas_call(
        functools.partial(network, count),
        out_shape=jax.ShapeDtypeStruct((mine, width), bf16),
        in_specs=[
            pl.BlockSpec(memory_space=pltpu.SMEM),
            pl.BlockSpec(memory_space=pl.ANY),
            pl.BlockSpec(memory_space=pl.ANY),
            pl.BlockSpec(memory_space=pl.ANY),
        ],
        out_specs=pl.BlockSpec(memory_space=pltpu.VMEM),
        scratch_shapes=[
            pltpu.VMEM((layers, pieces, owned, slots, side, side), bf16),
            pltpu.VMEM((mine, width), bf16),
            pltpu.VMEM(bias.shape, f32),
            pltpu.VMEM((CHUNKS, count, blocks // stack, height, side), bf16),
            pltpu.VMEM((CHUNKS, blocks + 1, height, side), bf16),
            pltpu.VMEM((blocks + 1, height, side), bf16),
            pltpu.VMEM((blocks + 1, height, side), bf16),
            pltpu.VMEM((layers, CHUNKS, 2, owned, height, side), f32),
            pltpu.VMEM((layers, CHUNKS, 2, owned, height, side), f32),
            pltpu.VMEM((layers, CHUNKS, owned, height, side), bf16),
            pltpu.VMEM((layers, CHUNKS, owned, height, side), bf16),
            pltpu.VMEM((owned, height, side), f32),
            pltpu.VMEM(turned, bf16),
            pltpu.VMEM(turned, bf16),
            dma((layers, pieces)),
            dma((2,)),
            dma((CHUNKS, 2, 5, PARTS)),
            dma((CHUNKS, 2, 5, PARTS)),
            dma((2, layers, CHUNKS, 2, PARTS)),
            dma((2, layers, CHUNKS, PARTS)),
            dma((2, CHUNKS, count)),
        ],
        compiler_params=pltpu.CompilerParams(
            collective_id=0, has_side_effects=True, vmem_limit_bytes=56 * 2**20
        ),
        name="network",
    )(picks, features, tiles.reshape(layers, pieces, owned, slots, side, side), bias)


def on_device(sizes, features, tiles, tile_rows, tile_counts, bias):
    count = sizes["row"]
    owned = tiles.shape[2]
    fits = (
        tiles.shape[0] == 2
        and sizes["col"] == 2
        and sizes["rep"] == 2
        and count == 4
        and features.shape[0] == 8
        and owned % (4 * PARTS) == 0
        and 2 * tiles[0].size * 2 <= 32 * 2**20
    )
    body = functools.partial(in_kernel, count) if fits else in_operations
    return body(features, tiles, tile_rows, tile_counts, bias)


def solution(mesh):
    in_specs = (
        P(("grp", "row"), ("col", "rep")),
        P(None, None, "row", ("col", "rep"), None, None, None),
        P(None, None, "row", ("col", "rep"), None),
        P(None, None, "row", ("col", "rep")),
        P(None, ("col", "rep")),
    )
    out_specs = P(("grp", "row"), ("col", "rep"))
    return jax.shard_map(
        functools.partial(on_device, dict(mesh.shape)),
        mesh=mesh, in_specs=in_specs, out_specs=out_specs, check_vma=False,
    )
```

```python
import functools

import jax
import jax.numpy as jnp
from jax import lax
from jax.experimental import pallas as pl
from jax.experimental.pallas import tpu as pltpu
from jax.sharding import PartitionSpec as P

MESH = pl.DeviceIdType.MESH
PARTS = 2
CHUNKS = 2


def partial_products(rows_x, tiles, tile_rows, tile_counts, layer):
    tile_width = tiles.shape[-1]
    out_count = tiles.shape[1] * tiles.shape[2]
    slots = tiles.shape[4]
    height = rows_x.shape[0]
    blocks = rows_x.reshape(height, -1, tile_width)
    picks = tile_rows[layer].reshape(-1)
    picked = jnp.take(blocks, picks, axis=1)
    live = lax.broadcasted_iota(jnp.int32, (out_count, slots), 1) < tile_counts[layer].reshape(
        out_count, 1
    )
    picked = (
        picked.reshape(height, out_count, slots, tile_width)
        * live.astype(jnp.bfloat16)[None, :, :, None]
    )
    weights = tiles[layer].reshape(out_count, slots, tile_width, tile_width)
    summed = jnp.einsum("rosd,osde->roe", picked, weights, preferred_element_type=jnp.float32)
    return summed.reshape(height, out_count * tile_width)


def finish(summed, bias, layer):
    partial_value = lax.psum_scatter(summed, ("col", "rep"), scatter_dimension=1, tiled=True)
    width = partial_value.shape[1]
    offset = lax.axis_index("row") * width
    shifts = lax.dynamic_slice_in_dim(bias[layer], offset, width)
    return jax.nn.relu(partial_value + shifts[None, :]).astype(jnp.bfloat16)


def in_operations(features, tiles, tile_rows, tile_counts, bias):
    layers = tiles.shape[0]
    rows_x = lax.all_gather(features, "row", axis=0, tiled=True)
    for layer in range(layers):
        finished = finish(partial_products(rows_x, tiles, tile_rows, tile_counts, layer), bias, layer)
        if layer + 1 < layers:
            rows_x = lax.all_gather(finished, "row", axis=1, tiled=True)
    return lax.all_to_all(finished, "row", split_axis=0, concat_axis=1, tiled=True)


class Line:
    MOVES = ((2, 2), (3, -2), (0, 1), (1, -1))
    ON = 4

    def __init__(self, count, place, sems):
        self.count, self.place, self.sems = count, place, sems
        self.me = lax.axis_index("row")

    def copy(self, slot, step, shard, part):
        ref = self.place(jnp.clip(shard, 0, self.count - 1), part)
        own = part if slot in (2, 3) and part is not None else 0
        return pltpu.make_async_remote_copy(
            src_ref=ref,
            dst_ref=ref,
            send_sem=self.sems.at[0, slot, 0],
            recv_sem=self.sems.at[1, slot, own],
            device_id={"row": jnp.clip(self.me + step, 0, self.count - 1)},
            device_id_type=MESH,
        )

    def inside(self, step):
        return self.me < self.count - step if step > 0 else self.me >= -step

    def start(self, part):
        for slot, step in self.MOVES:

            @pl.when(self.inside(step))
            def _():
                self.copy(slot, step, self.me, part).start()

    def hand_on(self, part):
        for place, slot, step, shard in ((1, 3, -1, 3), (2, 2, 1, 0)):

            @pl.when(self.me == place)
            def _():
                self.copy(slot, step, shard, part).wait_recv()
                self.copy(self.ON, step, shard, part).start()

    def wait(self):
        for slot, step in self.MOVES:
            came = self.inside(-step)
            if abs(step) == 2:
                came = came & ((self.me == 0) | (self.me == self.count - 1))

            @pl.when(came)
            def _():
                back = 1 if step < 0 else -1
                if abs(step) == 2:
                    each_part(lambda part: self.copy(slot, back, self.me - step, part).wait_recv())
                else:
                    self.copy(slot, back, self.me - step, None).wait_recv()

        for place, step, shard in ((0, 1, 3), (3, -1, 0)):

            @pl.when(self.me == place)
            def _():
                self.copy(self.ON, step, shard, None).wait_recv()

    def drain(self):
        for slot, step in self.MOVES:

            @pl.when(self.inside(step))
            def _():
                self.copy(slot, step, self.me, None).wait_send()

        for place, step, shard in ((1, -1, 3), (2, 1, 0)):

            @pl.when(self.me == place)
            def _():
                self.copy(self.ON, step, shard, None).wait_send()


def each_part(body):
    def step(part, carry):
        body(part)
        return carry

    lax.fori_loop(0, PARTS, step, 0)


def network(
    count, picks_ref, features_ref, tiles_ref, bias_ref, out_ref,
    weights, given, shifts, raw, x_first, x_second_low, x_second_high, sib_out, sib_in, far_out, far_in, total, turn_out, turn_in,
    weight_sem, load_sem, gather_sem, spread_sem, sib_sem, far_sem, turn_sem,
):
    layers, pieces, owned, slots, side, _ = weights.shape
    row, col, rep = (lax.axis_index(name) for name in ("row", "col", "rep"))
    chunks, slabs, height = raw.shape[0], raw.shape[2], raw.shape[3]
    piece_rows = height // count
    stack = height // piece_rows
    each = owned // PARTS
    f32, bf16 = jnp.float32, jnp.bfloat16

    x_second = (x_second_low, x_second_high)
    take_features = pltpu.make_async_copy(features_ref, given, load_sem.at[0])
    take_bias = pltpu.make_async_copy(bias_ref, shifts, load_sem.at[1])
    take_features.start()

    def load_weights(layer, piece):
        return pltpu.make_async_copy(
            tiles_ref.at[layer, piece], weights.at[layer, piece], weight_sem.at[layer, piece]
        )

    barrier = pltpu.get_barrier_semaphore()
    for away in range(1, count):
        pl.semaphore_signal(
            barrier, inc=1, device_id={"row": lax.rem(row + away, count)}, device_id_type=MESH
        )
    pl.semaphore_signal(barrier, inc=1, device_id={"rep": 1 - rep}, device_id_type=MESH)
    pl.semaphore_signal(barrier, inc=1, device_id={"col": 1 - col}, device_id_type=MESH)

    order = [(1 - col) * 2 + 1 - rep, (1 - col) * 2 + rep, col * 2 + 1 - rep, col * 2 + rep]
    take_features.wait()
    for layer in range(layers):
        for piece in order:
            load_weights(layer, piece).start()
    take_bias.start()

    def columns(block):
        return pl.ds(pl.multiple_of(block * side, side), side)

    def pack(chunk):
        rows = slice(chunk * piece_rows, (chunk + 1) * piece_rows)

        def step(at, carry):
            values = [given[:, columns(at + j * slabs)].astype(f32) for j in range(stack)]
            raw[chunk, row, at] = jnp.concatenate([v[rows] for v in values], axis=0).astype(bf16)
            return carry

        lax.fori_loop(0, slabs, step, 0, unroll=4)

    pack(0)
    pl.semaphore_wait(barrier, count + 1)

    def some(part, size, whole, base=0):
        return pl.ds(base, whole) if part is None else pl.ds(base + part * size, size)

    share = slabs // PARTS
    gathers, spreads = [], []
    for chunk in range(chunks):

        def raw_place(shard, part, chunk=chunk):
            return raw.at[chunk, shard, some(part, share, slabs)]

        def second_place(shard, part, chunk=chunk):
            return x_second[chunk].at[some(part, each, owned, shard * owned)]

        gathers.append(Line(count, raw_place, gather_sem.at[chunk]))
        spreads.append(Line(count, second_place, spread_sem.at[chunk]))
    each_part(gathers[0].start)
    for chunk in range(1, chunks):
        pack(chunk)
        each_part(gathers[chunk].start)
    for chunk in range(chunks):
        for x in (x_first.at[chunk], x_second[chunk]):
            x[stack * slabs] = jnp.zeros(x.shape[1:], bf16)

    def unpack(chunk):
        def step(at, carry):
            values = [raw[chunk, shard, at].astype(f32) for shard in range(count)]
            for j in range(stack):
                rows = slice(j * piece_rows, (j + 1) * piece_rows)
                block = jnp.concatenate([v[rows] for v in values], axis=0).astype(bf16)
                x_first[chunk, at + j * slabs] = block
            return carry

        lax.fori_loop(0, slabs, step, 0, unroll=4)

    def sib_copy(layer, chunk, which, part):
        at = some(part, each, owned)
        return pltpu.make_async_remote_copy(
            src_ref=sib_out.at[layer, chunk, which, at],
            dst_ref=sib_in.at[layer, chunk, which, at],
            send_sem=sib_sem.at[0, layer, chunk, which, 0],
            recv_sem=sib_sem.at[1, layer, chunk, which, 0 if part is None else part],
            device_id={"rep": 1 - rep},
            device_id_type=MESH,
        )

    def far_copy(layer, chunk, part):
        at = some(part, each, owned)
        return pltpu.make_async_remote_copy(
            src_ref=far_out.at[layer, chunk, at],
            dst_ref=far_in.at[layer, chunk, at],
            send_sem=far_sem.at[0, layer, chunk, 0],
            recv_sem=far_sem.at[1, layer, chunk, 0 if part is None else part],
            device_id={"col": 1 - col},
            device_id_type=MESH,
        )

    per_part = each // stack

    def turn_copy(chunk, away, part, sender):
        target = lax.rem(row + away, count)
        at = some(part, per_part, owned // stack)
        return pltpu.make_async_remote_copy(
            src_ref=turn_out.at[chunk, target, at],
            dst_ref=turn_in.at[chunk, sender, at],
            send_sem=turn_sem.at[0, chunk, away],
            recv_sem=turn_sem.at[1, chunk, away],
            device_id={"row": target},
            device_id_type=MESH,
        )

    def run(layer, chunk, beside):
        x = x_first.at[chunk] if layer == 0 else x_second[chunk]

        def ready(piece):
            if chunk == 0:
                load_weights(layer, piece).wait()

        def product(piece, block):
            first = ((layer * pieces + piece) * owned + block) * slots
            picked = [x[picks_ref[first + slot]] for slot in range(slots)]
            tile = weights[layer, piece, block].reshape(slots * side, side)
            return jnp.dot(jnp.concatenate(picked, axis=1), tile, preferred_element_type=f32)

        def for_sibling(which, piece):
            ready(piece)

            def step(part):
                for k in range(each):
                    block = part * each + k
                    sib_out[layer, chunk, which, block] = product(piece, block)
                sib_copy(layer, chunk, which, part).start()

            each_part(step)

        for_sibling(0, order[0])
        ready(order[1])

        def for_far(part):
            sib_copy(layer, chunk, 0, part).wait_recv()
            for k in range(each):
                block = part * each + k
                value = product(order[1], block) + sib_in[layer, chunk, 0, block]
                far_out[layer, chunk, block] = value.astype(bf16)
            far_copy(layer, chunk, part).start()
            if beside is not None:
                beside.hand_on(part)

        each_part(for_far)
        for_sibling(1, order[2])
        ready(order[3])

        def own(part):
            sib_copy(layer, chunk, 1, part).wait_recv()
            for k in range(each):
                block = part * each + k
                total[block] = product(order[3], block) + sib_in[layer, chunk, 1, block]

        each_part(own)

        def done(block):
            shift = shifts[layer : layer + 1, columns(row * owned + block)]
            value = total[block] + far_in[layer, chunk, block].astype(f32) + shift
            return jnp.maximum(value, 0.0)

        def close(part):
            far_copy(layer, chunk, part).wait_recv()
            if layer + 1 < layers:
                for k in range(each):
                    block = part * each + k
                    x_second[chunk][row * owned + block] = done(block).astype(bf16)
                spreads[chunk].start(part)
            else:
                for k in range(per_part):
                    at = part * per_part + k
                    values = [done(part * each + j * per_part + k) for j in range(stack)]
                    for target in range(count):
                        rows = slice(target * piece_rows, (target + 1) * piece_rows)
                        slab = jnp.concatenate([v[rows] for v in values], axis=0).astype(bf16)
                        turn_out[chunk, target, at] = slab
                for away in range(1, count):
                    turn_copy(chunk, away, part, row).start()

        each_part(close)

    def settle(layer, chunk):
        far_copy(layer, chunk, None).wait_send()
        for which in range(2):
            sib_copy(layer, chunk, which, None).wait_send()
        if layer + 1 == layers:
            for away in range(1, count):
                turn_copy(chunk, away, None, row).wait_send()

    each_part(gathers[0].hand_on)
    gathers[0].wait()
    unpack(0)
    take_bias.wait()
    run(0, 0, gathers[1])
    gathers[1].wait()
    unpack(1)
    run(0, 1, spreads[0])
    spreads[0].wait()
    run(1, 0, spreads[1])
    for chunk in range(chunks):
        gathers[chunk].drain()
        settle(0, chunk)
    settle(1, 0)
    spreads[0].drain()
    spreads[1].wait()
    run(1, 1, None)
    spreads[1].drain()

    def put_all(sender, source, index):
        def step(at, carry):
            values = [source[chunk, index, at].astype(f32) for chunk in range(chunks)]
            for j in range(stack):
                rows = slice(j * piece_rows, (j + 1) * piece_rows)
                block = sender * owned + (at // per_part) * each + j * per_part + at % per_part
                both = jnp.concatenate([v[rows] for v in values], axis=0)
                out_ref[:, columns(block)] = both.astype(bf16)
            return carry

        lax.fori_loop(0, owned // stack, step, 0, unroll=4)

    put_all(row, turn_out, row)
    for away in range(1, count):
        sender = lax.rem(row + count - away, count)
        for chunk in range(chunks):
            turn_copy(chunk, away, None, sender).wait_recv()
        put_all(sender, turn_in, sender)
    settle(1, 1)


def in_kernel(count, features, tiles, tile_rows, tile_counts, bias):
    layers, pieces, owned, _, slots, side, _ = tiles.shape
    mine, width = features.shape
    blocks = width // side
    height = mine * count // CHUNKS
    stack = count
    live = lax.broadcasted_iota(jnp.int32, tile_rows.shape, 4) < tile_counts[..., None]
    picks = jnp.where(live, tile_rows, blocks).reshape(-1)
    f32, bf16, dma = jnp.float32, jnp.bfloat16, pltpu.SemaphoreType.DMA
    turned = (CHUNKS, count, owned // stack, height, side)
    return pl.pallas_call(
        functools.partial(network, count),
        out_shape=jax.ShapeDtypeStruct((mine, width), bf16),
        in_specs=[
            pl.BlockSpec(memory_space=pltpu.SMEM),
            pl.BlockSpec(memory_space=pl.ANY),
            pl.BlockSpec(memory_space=pl.ANY),
            pl.BlockSpec(memory_space=pl.ANY),
        ],
        out_specs=pl.BlockSpec(memory_space=pltpu.VMEM),
        scratch_shapes=[
            pltpu.VMEM((layers, pieces, owned, slots, side, side), bf16),
            pltpu.VMEM((mine, width), bf16),
            pltpu.VMEM(bias.shape, f32),
            pltpu.VMEM((CHUNKS, count, blocks // stack, height, side), bf16),
            pltpu.VMEM((CHUNKS, blocks + 1, height, side), bf16),
            pltpu.VMEM((blocks + 1, height, side), bf16),
            pltpu.VMEM((blocks + 1, height, side), bf16),
            pltpu.VMEM((layers, CHUNKS, 2, owned, height, side), f32),
            pltpu.VMEM((layers, CHUNKS, 2, owned, height, side), f32),
            pltpu.VMEM((layers, CHUNKS, owned, height, side), bf16),
            pltpu.VMEM((layers, CHUNKS, owned, height, side), bf16),
            pltpu.VMEM((owned, height, side), f32),
            pltpu.VMEM(turned, bf16),
            pltpu.VMEM(turned, bf16),
            dma((layers, pieces)),
            dma((2,)),
            dma((CHUNKS, 2, 5, PARTS)),
            dma((CHUNKS, 2, 5, PARTS)),
            dma((2, layers, CHUNKS, 2, PARTS)),
            dma((2, layers, CHUNKS, PARTS)),
            dma((2, CHUNKS, count)),
        ],
        compiler_params=pltpu.CompilerParams(
            collective_id=0, has_side_effects=True, vmem_limit_bytes=40 * 2**20
        ),
        name="network",
    )(picks, features, tiles.reshape(layers, pieces, owned, slots, side, side), bias)


def on_device(sizes, features, tiles, tile_rows, tile_counts, bias):
    count = sizes["row"]
    owned = tiles.shape[2]
    fits = (
        tiles.shape[0] == 2
        and sizes["col"] == 2
        and sizes["rep"] == 2
        and count == 4
        and features.shape[0] == 8
        and owned % (4 * PARTS) == 0
        and 2 * tiles[0].size * 2 <= 32 * 2**20
    )
    body = functools.partial(in_kernel, count) if fits else in_operations
    return body(features, tiles, tile_rows, tile_counts, bias)


def solution(mesh):
    in_specs = (
        P(("grp", "row"), ("col", "rep")),
        P(None, None, "row", ("col", "rep"), None, None, None),
        P(None, None, "row", ("col", "rep"), None),
        P(None, None, "row", ("col", "rep")),
        P(None, ("col", "rep")),
    )
    out_specs = P(("grp", "row"), ("col", "rep"))
    return jax.shard_map(
        functools.partial(on_device, dict(mesh.shape)),
        mesh=mesh, in_specs=in_specs, out_specs=out_specs, check_vma=False,
    )
```
